32 devices in a mesh: groups: 2 (over y), gx: 4 (over z), gy: 2 (over x), gz: 2 (over core).
Axes of the slice: x: 2, y: 2, z: 4, core: 2. Of those that a mesh axis runs over, the one named last changes fastest.
Arguments:
- wave_state: float32 [18, 4, 64, 256], P('groups', 'gz', 'gx', 'gy'), parts along dimension 0, may hold values from -6 to 6
- buoyancy: float32 [8, 64, 256], P(('groups', 'gz'), 'gx', 'gy'), parts along dimension 0, may hold values from 0.5 to 2
- sponge_level: int32 [8, 64, 256], P(('groups', 'gz'), 'gx', 'gy'), parts along dimension 0, may hold values from 0 to 6, as said below
- spins: float32 [6, 8, 64, 256], P('groups', 'gz', 'gx', 'gy'), parts along dimension 0, as said below
- regions: int32 [128, 2], P(('groups', 'gx'), 'gy'), parts along dimension 0, may hold values from 0 to 3
- region_table: float32 [4, 4], replicated, may hold values from 0.3 to 1.5
Outputs:
- wave_out: float32 [18, 4, 64, 256], P('groups', 'gz', 'gx', 'gy'), parts along dimension 0
- spins_out: float32 [6, 8, 64, 256], P('groups', 'gz', 'gx', 'gy'), parts along dimension 0
The draws below stay inside these ranges and needn't reach their ends.
There are 2 independent parts, one for each index of `groups`. The reference program is written for one: setup_inputs(seed, part) draws one part's arguments, and reference() takes and returns one part's arrays. A program takes and returns all parts, laid end to end along the dimension named above; an argument that names none is the same for every part. Nothing has to cross between parts.
Inputs may be any that keep to these rules, and one draw needn't show every extreme that they name: `sponge_level`: levels are highest at the lateral edges and fall inward. `spins`: each cell's three components form a vector of length one.
All inputs are finite; a program needn't handle non-finite values.
Results may differ from the reference program's by a relative error of at most 0.00026.
Values sent between devices are 32-bit elements; how exact they have to be, the bound alone decides.
A program may use at most 64 MiB of HBM per device.

```python
import math
import jax
import jax.numpy as jnp
from jax import lax

FL = 8
TILE = 128
REGIONS = 4
SPONGE_MAX = 6
SUBSTEPS = 4
LLG_STEPS = 2
NX = 64
NY = 256
NZ = 4


def draw_sponge_level(key, part):
    key = jax.random.fold_in(key, 11)
    x_index = jnp.arange(NX, dtype=jnp.int32)
    y_index = jnp.arange(NY, dtype=jnp.int32)
    x_distance = jnp.minimum(x_index, NX - 1 - x_index)
    y_distance = jnp.minimum(y_index, NY - 1 - y_index)
    distance = jnp.minimum(x_distance[:, None], y_distance[None, :])
    jitter = jax.random.randint(key, (NZ, NX, NY), 0, 2).astype(jnp.int32)
    jitter = jnp.where(distance[None] == 0, 0, jitter)
    return jnp.clip(SPONGE_MAX - distance[None] - jitter, 0, SPONGE_MAX).astype(jnp.int32)


def draw_spins(key, part):
    key = jax.random.fold_in(key, 23)
    key_height, key_angle = jax.random.split(key)
    height = jax.random.uniform(key_height, (FL, NX, NY), jnp.float32, -1.0, 1.0)
    azimuth = jax.random.uniform(key_angle, (FL, NX, NY), jnp.float32, -math.pi, math.pi)
    radial = jnp.sqrt(jnp.maximum(1.0 - height * height, 0.0))
    return jnp.stack([radial * jnp.cos(azimuth), radial * jnp.sin(azimuth), height]).astype(jnp.float32)


def touch_ends(result, stream_key, smallest, top_value):
    spot = [jax.random.randint(jax.random.fold_in(stream_key, axis), (), 0, length) for axis, length in enumerate(result.shape)]
    longest = result.shape.index(max(result.shape))
    beside = spot[:longest] + [(spot[longest] + 1) % result.shape[longest]] + spot[longest + 1:]
    return result.at[tuple(spot)].set(smallest).at[tuple(beside)].set(top_value)


def steps_of(rng, shape, pieces, low, top_value):
    gain = 1.0
    for position, shards_of in pieces:
        draws = jax.random.uniform(jax.random.fold_in(jax.random.fold_in(rng, 6), position), (shards_of,), jnp.float32, low / len(pieces), top_value / len(pieces))
        gain = gain * jnp.repeat(jnp.exp(draws), shape[position] // shards_of).reshape((-1,) + (1,) * (len(shape) - 1 - position))
    return gain


def scatter_about(rng, shape, scale, reach, shards=(), kind=jnp.bfloat16):
    gain = steps_of(rng, shape, shards, -0.22, 0.18) if shards else 1.0
    values = jax.random.normal(rng, shape, jnp.float32) * scale * gain
    return jnp.minimum(jnp.maximum(values, -reach), reach).astype(kind)


def setup_inputs(seed: int = 0, part: int = 0) -> dict:
    arg_keys = jax.random.split(jax.random.key(seed), 7)
    part_splits = jax.random.split(jax.random.fold_in(arg_keys[6], part), 7)
    return {
        "wave_state": scatter_about(part_splits[0], (9, NZ, NX, NY), 1.0, 6.0, ((1, 2), (2, 4), (3, 2)), jnp.float32),
        "buoyancy": jnp.clip(jnp.exp(math.log(2.0) - 1.3862944 * jax.random.uniform(part_splits[1], (NZ, NX, NY), jnp.float32) ** steps_of(part_splits[1], (NZ, NX, NY), ((0, 2), (1, 4), (2, 2)), -0.2, 0.2)), 0.5, 2.0),
        "sponge_level": draw_sponge_level(jax.random.fold_in(jax.random.fold_in(arg_keys[6], part), 71), part),
        "spins": draw_spins(jax.random.fold_in(jax.random.fold_in(arg_keys[6], part), 71), part),
        "regions": touch_ends(jax.random.randint(part_splits[4], (NX, NY // TILE), 0, REGIONS), jax.random.fold_in(part_splits[4], 1), 0, REGIONS - 1).astype(jnp.int32),
        "region_table": jnp.clip(jax.random.uniform(arg_keys[5], (4, REGIONS), jnp.float32, 0.3, 1.5), 0.3, 1.5),
    }


LAME_FIRST = 1.0
LAME_SHEAR = 1.0
ELASTIC_STEP = 0.3
SPIN_STEP = 0.04
DAMPING = 0.3
FORCE_SCALE = 0.25
SPONGE_RATE = 0.08
POISSON = LAME_FIRST / (3.0 * LAME_FIRST + 2.0 * LAME_SHEAR)

def derive(field, which_axis):
    padding = [(0, 0)] * field.ndim
    padding[which_axis] = (1, 1)
    padded = jnp.pad(field, padding)
    extent = field.shape[which_axis]
    upper_part = lax.slice_in_dim(padded, 2, extent + 2, axis=which_axis)
    lower_part = lax.slice_in_dim(padded, 0, extent, axis=which_axis)
    return 0.5 * (upper_part - lower_part)

def elastic_step(velocity, stresses, buoyant, damping_factor, surface_force):

    def grad_stress(component, which_axis):
        return derive(stresses[component], which_axis)
    divergence = jnp.stack([grad_stress(0, 1) + grad_stress(5, 2) + grad_stress(4, 0), grad_stress(5, 1) + grad_stress(1, 2) + grad_stress(3, 0), grad_stress(4, 1) + grad_stress(3, 2) + grad_stress(2, 0)])
    divergence = divergence.at[:, 0].add(surface_force)
    velocity = damping_factor * (velocity + ELASTIC_STEP * buoyant * divergence)

    def grad_velocity(component, which_axis):
        return derive(velocity[component], which_axis)
    strain_xx = grad_velocity(0, 1)
    strain_yy = grad_velocity(1, 2)
    strain_zz = grad_velocity(2, 0)
    trace = strain_xx + strain_yy + strain_zz
    stress_rate = jnp.stack([LAME_FIRST * trace + 2.0 * LAME_SHEAR * strain_xx, LAME_FIRST * trace + 2.0 * LAME_SHEAR * strain_yy, LAME_FIRST * trace + 2.0 * LAME_SHEAR * strain_zz, LAME_SHEAR * (grad_velocity(1, 0) + grad_velocity(2, 2)), LAME_SHEAR * (grad_velocity(0, 0) + grad_velocity(2, 1)), LAME_SHEAR * (grad_velocity(0, 2) + grad_velocity(1, 1))])
    stresses = damping_factor * (stresses + ELASTIC_STEP * stress_rate)
    return (velocity, stresses)

def spin_step(extended, surface, anisotropy, chirality, normal_couple, shear_couple):
    centre = extended[:, 1:-1, 1:-1, 1:-1]
    laplace = extended[:, 2:, 1:-1, 1:-1] + extended[:, :-2, 1:-1, 1:-1] + extended[:, 1:-1, 2:, 1:-1] + extended[:, 1:-1, :-2, 1:-1] + extended[:, 1:-1, 1:-1, 2:] + extended[:, 1:-1, 1:-1, :-2] - 6.0 * centre
    along_x = 0.5 * (extended[:, 1:-1, 2:, 1:-1] - extended[:, 1:-1, :-2, 1:-1])
    along_y = 0.5 * (extended[:, 1:-1, 1:-1, 2:] - extended[:, 1:-1, 1:-1, :-2])
    trace = surface[0] + surface[1] + surface[2]
    strain_xx = (surface[0] - POISSON * trace) / (2.0 * LAME_SHEAR)
    strain_yy = (surface[1] - POISSON * trace) / (2.0 * LAME_SHEAR)
    strain_zz = (surface[2] - POISSON * trace) / (2.0 * LAME_SHEAR)
    strain_yz = surface[3] / (2.0 * LAME_SHEAR)
    strain_xz = surface[4] / (2.0 * LAME_SHEAR)
    strain_xy = surface[5] / (2.0 * LAME_SHEAR)
    spin_x, spin_y, spin_z = (centre[0], centre[1], centre[2])
    coupled_x = -2.0 * normal_couple * strain_xx * spin_x - 2.0 * shear_couple * (strain_xy * spin_y + strain_xz * spin_z)
    coupled_y = -2.0 * normal_couple * strain_yy * spin_y - 2.0 * shear_couple * (strain_xy * spin_x + strain_yz * spin_z)
    coupled_z = -2.0 * normal_couple * strain_zz * spin_z - 2.0 * shear_couple * (strain_xz * spin_x + strain_yz * spin_y)
    field_x = laplace[0] + chirality * along_x[2] + coupled_x
    field_y = laplace[1] + chirality * along_y[2] + coupled_y
    field_z = laplace[2] - chirality * (along_x[0] + along_y[1]) + 2.0 * anisotropy * spin_z + coupled_z
    torque_x = spin_y * field_z - spin_z * field_y
    torque_y = spin_z * field_x - spin_x * field_z
    torque_z = spin_x * field_y - spin_y * field_x
    relax_x = spin_y * torque_z - spin_z * torque_y
    relax_y = spin_z * torque_x - spin_x * torque_z
    relax_z = spin_x * torque_y - spin_y * torque_x
    factor = SPIN_STEP / (1.0 + DAMPING * DAMPING)
    moved = jnp.stack([spin_x - factor * (torque_x + DAMPING * relax_x), spin_y - factor * (torque_y + DAMPING * relax_y), spin_z - factor * (torque_z + DAMPING * relax_z)])
    length_now = jnp.sqrt(moved[0] * moved[0] + moved[1] * moved[1] + moved[2] * moved[2])
    return moved / length_now

def film_push(film_spins, normal_couple, shear_couple):
    spin_x, spin_y, spin_z = (film_spins[0], film_spins[1], film_spins[2])
    return FORCE_SCALE * jnp.stack([shear_couple * lax.optimization_barrier(jnp.sum(spin_x * spin_z, axis=0)), shear_couple * lax.optimization_barrier(jnp.sum(spin_y * spin_z, axis=0)), normal_couple * lax.optimization_barrier(jnp.sum(spin_z * spin_z - 1.0 / 3.0, axis=0))])

def reference(wave_state, buoyancy, sponge_level, spins, regions, region_table):
    damping_factor = 1.0 - SPONGE_RATE * sponge_level.astype(jnp.float32)
    region_cells = jnp.repeat(regions, TILE, axis=1)
    material = region_table[:, region_cells]
    velocity, stresses = (wave_state[:3], wave_state[3:])
    film_spins = spins
    for llg_step in range(LLG_STEPS):
        surface = stresses[:, 0]
        extended = jnp.pad(film_spins, ((0, 0), (1, 1), (1, 1), (1, 1)), mode='edge')
        film_spins = spin_step(extended, surface, material[0], material[1], material[2], material[3])
        surface_force = film_push(film_spins, material[2], material[3])
        for sub_step in range(SUBSTEPS):
            velocity, stresses = elastic_step(velocity, stresses, buoyancy, damping_factor, surface_force)
    return (jnp.concatenate([velocity, stresses], axis=0), film_spins)
```

```python
import functools

import jax
import jax.numpy as jnp
from jax import lax
from jax.experimental import pallas as pl
from jax.experimental.pallas import tpu as pltpu
from jax.sharding import PartitionSpec as P

SUBSTEPS = 4
LLG_STEPS = 2
REACH = 2 * SUBSTEPS * LLG_STEPS
PAD = 8
ELASTIC_STEP = 0.3
SPIN_STEP = 0.04
DAMPING = 0.3
FORCE_SCALE = 0.25
SPONGE_RATE = 0.08
POISSON = 0.2
MESH = pl.DeviceIdType.MESH


def kernel(
    sizes,
    wave, buoy, sponge, spin, regions, table,
    wave_out, spin_out,
    W, B, G, A, F, M, MAT, K, FORCE, PKS, PKR, MOWN, WX, FX,
    xs_sem, xr_sem, ps_sem, pr_sem, fs_sem, fr_sem, ys_sem, yr_sem, os_sem, or_sem, l_sem,
):
    n_x, n_y = sizes
    g = lax.axis_index("groups")
    x = lax.axis_index("gx")
    y = lax.axis_index("gy")
    h = lax.axis_index("gz")
    rows = wave.shape[2]
    halo = REACH
    depth = wave.shape[1]
    layers = spin.shape[1]
    lo0, own0, hi0 = PAD, PAD + halo, PAD + halo + rows
    total = rows + 2 * halo
    span = slice(PAD, PAD + total)
    own = slice(own0, own0 + rows)

    partner = (g, x, y, 1 - h)
    has_lo, has_hi = x > 0, x < n_x - 1
    has_left, has_right = y > 0, y < n_y - 1
    step_y = 1 - 2 * h
    y_to = y + step_y
    y_from = y - step_y
    sends_y = jnp.logical_and(y_to >= 0, y_to < n_y)
    takes_y = jnp.logical_and(y_from >= 0, y_from < n_y)

    barrier = pltpu.get_barrier_semaphore()

    def greet(cond, dev):
        @pl.when(cond)
        def _():
            pl.semaphore_signal(barrier, inc=1, device_id=dev, device_id_type=MESH)

    pl.semaphore_signal(barrier, inc=1, device_id=partner, device_id_type=MESH)
    greet(has_lo, (g, x - 1, y, h))
    greet(has_hi, (g, x + 1, y, h))
    greet(has_left, (g, x, y - 1, h))
    greet(has_right, (g, x, y + 1, h))

    lane_own = lax.broadcasted_iota(jnp.int32, (rows, 128), 1)
    region = jnp.broadcast_to(regions[...], (rows, 128))
    packed = jnp.zeros((rows, 128), jnp.float32)
    for p in range(4):
        value = jnp.zeros((rows, 128), jnp.float32)
        for r in range(table.shape[1]):
            value = jnp.where(region == r, table[p, r], value)
        packed = jnp.where(lane_own // 32 == p, value, packed)
    MOWN[...] = packed

    i32 = lambda c: jnp.where(c, 1, 0).astype(jnp.int32)
    pl.semaphore_wait(barrier, 1 + i32(has_lo) + i32(has_hi) + i32(has_left) + i32(has_right))

    d0 = 1 + depth * h
    b0 = depth * h
    f0 = layers * h

    def piece(i, r):
        rr = pl.ds(r, rows)
        return [
            (spin, F.at[0, :, pl.ds(f0, layers), rr]),
            (MOWN, M.at[rr]),
            (wave.at[3:9, 0:1], W.at[3:9, pl.ds(d0, 1), rr]),
            (wave.at[0:3], W.at[0:3, pl.ds(d0, depth), rr]),
            (wave.at[3:9, 1:depth], W.at[3:9, pl.ds(d0 + 1, depth - 1), rr]),
            (buoy, B.at[pl.ds(b0, depth), rr]),
            (sponge, G.at[pl.ds(b0, depth), rr]),
        ][i]

    count = 7
    with_partner = (0, 2, 3, 4, 5, 6)
    group_a, group_b = (0, 1, 2), (3, 4, 5, 6)

    def x_copy(i, up):
        src, dst = piece(i, lo0 if up else hi0)
        return pltpu.make_async_remote_copy(
            src_ref=src, dst_ref=dst, send_sem=xs_sem.at[i, 0 if up else 1],
            recv_sem=xr_sem.at[i, 0 if up else 1],
            device_id=(g, x + 1 if up else x - 1, y, h), device_id_type=MESH)

    def own_copy(i):
        src, dst = piece(i, own0)
        return pltpu.make_async_remote_copy(
            src_ref=src, dst_ref=dst, send_sem=ps_sem.at[i], recv_sem=pr_sem.at[i],
            device_id=partner, device_id_type=MESH)

    def forward(i, low):
        _, dst = piece(i, lo0 if low else hi0)
        k = 0 if low else 1
        return pltpu.make_async_remote_copy(
            src_ref=dst, dst_ref=dst, send_sem=fs_sem.at[i, k], recv_sem=fr_sem.at[i, k],
            device_id=partner, device_id_type=MESH)

    def local_copy(i):
        src, dst = piece(i, own0)
        return pltpu.make_async_copy(src, dst, l_sem.at[i])

    for i in range(count):
        @pl.when(has_hi)
        def _():
            x_copy(i, True).start()

        @pl.when(has_lo)
        def _():
            x_copy(i, False).start()

    for i in range(count):
        if i in with_partner:
            own_copy(i).start()
        local_copy(i).start()

    zero_row = jnp.zeros((PAD, 128), jnp.float32)

    for c in range(9):
        for d in (0, 1 + 2 * depth):
            W[c, d] = jnp.zeros((total + 2 * PAD, 128), jnp.float32)

    def pad_rows(d, carry):
        for c in range(9):
            W[c, d, 0:PAD] = zero_row
            W[c, d, PAD + total:] = zero_row
        return carry

    lax.fori_loop(1, 1 + 2 * depth, pad_rows, 0)

    def pad_film(l, carry):
        for c in range(3):
            for b in range(2):
                F[b, c, l, 0:PAD] = zero_row
                F[b, c, l, PAD + total:] = zero_row
        return carry

    lax.fori_loop(0, 2 * layers, pad_film, 0)
    for c in range(3):
        for d in range(1, 2 * depth):
            FORCE[d, c] = jnp.zeros((total, 128), jnp.float32)

    @pl.when(jnp.logical_not(takes_y))
    def _():
        PKR[...] = jnp.zeros_like(PKR)

    lane = lax.broadcasted_iota(jnp.int32, (total, 128), 1)
    row = lax.broadcasted_iota(jnp.int32, (total, 128), 0)
    slot = lax.rem(lane // 16 + (1 - h), 8)
    halo_lane = slot == 0
    halo_film = jnp.logical_and(halo_lane, takes_y)

    def arrive(group):
        for i in group:
            @pl.when(has_lo)
            def _():
                x_copy(i, True).wait_recv()
                if i in with_partner:
                    forward(i, True).start()

            @pl.when(has_hi)
            def _():
                x_copy(i, False).wait_recv()
                if i in with_partner:
                    forward(i, False).start()

        for i in group:
            local_copy(i).wait()
            if i in with_partner:
                own_copy(i).wait_recv()

                @pl.when(has_lo)
                def _():
                    forward(i, True).wait_recv()

                @pl.when(has_hi)
                def _():
                    forward(i, False).wait_recv()

    def sent(group):
        for i in group:
            if i in with_partner:
                own_copy(i).wait_send()

            @pl.when(has_hi)
            def _():
                x_copy(i, True).wait_send()
                if i in with_partner:
                    forward(i, False).wait_send()

            @pl.when(has_lo)
            def _():
                x_copy(i, False).wait_send()
                if i in with_partner:
                    forward(i, True).wait_send()

    def fill(refs, cond, r, zero):
        rr = slice(r, r + rows)

        @pl.when(jnp.logical_not(cond))
        def _():
            for ref in refs:
                ref[..., rr, :] = jnp.zeros_like(ref[..., rr, :]) if zero else ref[..., own, :]

    def pack(planes, first):
        for k in range(0, len(planes), 8):
            out = jnp.zeros((total, 128), jnp.float32)
            for j, ref in enumerate(planes[k:k + 8]):
                value = ref[span]
                if j:
                    value = pltpu.roll(value, 16 * j, 1)
                out = jnp.where(slot == j, value, out)
            PKS[first + k // 8] = out

    def unpack(planes, first, mask):
        for k in range(0, len(planes), 8):
            got = PKR[first + k // 8]
            for j, ref in enumerate(planes[k:k + 8]):
                value = pltpu.roll(got, 128 - 16 * j, 1) if j else got
                ref[span] = jnp.where(mask, value, ref[span])

    film_planes = [F.at[0, c, l] for c in range(3) for l in range(2 * layers)]
    stress = range(3, 9)
    first_stress = [W.at[c, 1] for c in stress] + [W.at[c, 1 + depth] for c in stress]
    rest = [W.at[c, 1 + d] for c in range(3) for d in range(2 * depth)]
    rest += [W.at[c, 1 + d] for c in stress for d in range(2 * depth) if d % depth]
    coefs = [B.at[d] for d in range(2 * depth)] + [A.at[d] for d in range(2 * depth)]
    early, late = first_stress[:8], first_stress[8:] + rest + coefs
    n_film = len(film_planes) // 8
    n_a = n_film + 2
    n_b = (len(late) + 7) // 8

    def y_copy(k):
        sl = pl.ds(0, n_a) if k == 0 else pl.ds(n_a, n_b)
        return pltpu.make_async_remote_copy(
            src_ref=PKS.at[sl], dst_ref=PKR.at[sl], send_sem=ys_sem.at[k], recv_sem=yr_sem.at[k],
            device_id=(g, x, y_to, h), device_id_type=MESH)

    def y_start(k):
        @pl.when(sends_y)
        def _():
            y_copy(k).start()

    def y_wait(k):
        @pl.when(sends_y)
        def _():
            y_copy(k).wait_send()

        @pl.when(takes_y)
        def _():
            y_copy(k).wait_recv()

    arrive(group_a)
    for cond, r in ((has_lo, lo0), (has_hi, hi0)):
        fill([F.at[0], M], cond, r, False)
        fill([W.at[3:9, 1:2], W.at[3:9, 1 + depth:2 + depth]], cond, r, True)
    pack(film_planes, 0)
    pack(early, n_film)
    PKS[n_film + 1] = M[span]
    y_start(0)

    arrive(group_b)
    for cond, r in ((has_lo, lo0), (has_hi, hi0)):
        fill([B], cond, r, False)
        fill([W.at[0:3, 1:1 + 2 * depth]], cond, r, True)
        for d in range(2 * depth):
            if d % depth:
                fill([W.at[3:9, 1 + d:2 + d]], cond, r, True)
    inside = jnp.logical_and(
        jnp.logical_or(row >= halo, has_lo), jnp.logical_or(row < halo + rows, has_hi))
    for d in range(2 * depth):
        A[d, span] = jnp.where(inside, 1.0 - SPONGE_RATE * G[d, span].astype(jnp.float32), 0.0)
    pack(late, n_a)
    y_start(1)

    sent(group_a)
    y_wait(0)
    unpack(film_planes, 0, halo_film)
    unpack(early, n_film, halo_lane)
    mine, other = M[span], PKR[n_film + 1]
    for p in range(4):
        at = slice(32 * p, 32 * p + 1)
        MAT[p] = jnp.where(
            halo_film, jnp.broadcast_to(other[:, at], (total, 128)),
            jnp.broadcast_to(mine[:, at], (total, 128)))

    def spin_step(now, r0, n):
        new = 1 - now
        rr, mm = slice(PAD + r0, PAD + r0 + n), slice(r0, r0 + n)
        s = [W[c, 1, rr] for c in stress]
        an, nc, sc = MAT[0, mm], MAT[2, mm], MAT[3, mm]
        part = POISSON * (s[0] + s[1] + s[2])
        K[0, mm] = -6.0 - nc * (s[0] - part)
        K[1, mm] = -6.0 - nc * (s[1] - part)
        K[2, mm] = -6.0 - nc * (s[2] - part) + 2.0 * an
        for q in (3, 4, 5):
            K[q, mm] = -(sc * s[q])
        lanes = lax.broadcasted_iota(jnp.int32, (n, 128), 1)
        at_rows = lax.broadcasted_iota(jnp.int32, (n, 128), 0) + r0
        x_first = jnp.logical_and(at_rows == halo, x == 0)
        x_last = jnp.logical_and(at_rows == halo + rows - 1, x == n_x - 1)
        y_first = jnp.logical_and(lanes == 0, jnp.logical_and(y == 0, h == 0))
        y_last = jnp.logical_and(lanes == 127, jnp.logical_and(y == n_y - 1, h == 1))
        factor = SPIN_STEP / (1.0 + DAMPING * DAMPING)

        def layer(l, sums):
            up, down = jnp.minimum(l + 1, 2 * layers - 1), jnp.maximum(l - 1, 0)
            m, lap, dx, dy = [], [], [], []
            for c in range(3):
                mid = F[now, c, l, rr]
                xp = jnp.where(x_last, mid, F[now, c, l, PAD + r0 + 1:PAD + r0 + 1 + n])
                xm = jnp.where(x_first, mid, F[now, c, l, PAD + r0 - 1:PAD + r0 - 1 + n])
                yp = jnp.where(y_last, mid, pltpu.roll(mid, 127, 1))
                ym = jnp.where(y_first, mid, pltpu.roll(mid, 1, 1))
                m.append(mid)
                lap.append(F[now, c, up, rr] + F[now, c, down, rr] + xp + xm + yp + ym)
                dx.append(xp - xm if c != 1 else None)
                dy.append(yp - ym if c != 0 else None)
            mx, my, mz = m
            half = 0.5 * MAT[1, mm]
            hx = lap[0] + half * dx[2] + K[0, mm] * mx + K[5, mm] * my + K[4, mm] * mz
            hy = lap[1] + half * dy[2] + K[5, mm] * mx + K[1, mm] * my + K[3, mm] * mz
            hz = lap[2] - half * (dx[0] + dy[1]) + K[4, mm] * mx + K[3, mm] * my + K[2, mm] * mz
            tx = my * hz - mz * hy
            ty = mz * hx - mx * hz
            tz = mx * hy - my * hx
            qx = mx - factor * (tx + DAMPING * (my * tz - mz * ty))
            qy = my - factor * (ty + DAMPING * (mz * tx - mx * tz))
            qz = mz - factor * (tz + DAMPING * (mx * ty - my * tx))
            square = qx * qx + qy * qy + qz * qz
            inv = lax.rsqrt(square)
            inv = inv * (1.5 - 0.5 * square * inv * inv)
            qx, qy, qz = qx * inv, qy * inv, qz * inv
            F[new, 0, l, rr] = qx
            F[new, 1, l, rr] = qy
            F[new, 2, l, rr] = qz
            return sums[0] + qx * qz, sums[1] + qy * qz, sums[2] + (qz * qz - 1.0 / 3.0)

        zero = jnp.zeros((n, 128), jnp.float32)
        sums = lax.fori_loop(0, 2 * layers, layer, (zero, zero, zero))
        sc, nc = MAT[3, mm], MAT[2, mm]
        FORCE[0, 0, mm] = (2.0 * FORCE_SCALE) * (sc * sums[0])
        FORCE[0, 1, mm] = (2.0 * FORCE_SCALE) * (sc * sums[1])
        FORCE[0, 2, mm] = (2.0 * FORCE_SCALE) * (nc * sums[2])

    def elastic(r0, n):
        lo = PAD + r0
        rr, mm = slice(lo, lo + n), slice(r0, r0 + n)

        def dx(c, d):
            return W[c, d, lo + 1:lo + 1 + n] - W[c, d, lo - 1:lo - 1 + n]

        def dy(c, d):
            value = W[c, d, rr]
            return pltpu.roll(value, 127, 1) - pltpu.roll(value, 1, 1)

        def dz(c, d):
            return W[c, d + 1, rr] - W[c, d - 1, rr]

        def velocity(k, carry):
            d = k + 1
            a, b = A[k, rr], B[k, rr]
            W[0, d, rr] = a * W[0, d, rr] + b * (dx(3, d) + dy(8, d) + dz(7, d) + FORCE[k, 0, mm])
            W[1, d, rr] = a * W[1, d, rr] + b * (dx(8, d) + dy(4, d) + dz(6, d) + FORCE[k, 1, mm])
            W[2, d, rr] = a * W[2, d, rr] + b * (dx(7, d) + dy(6, d) + dz(5, d) + FORCE[k, 2, mm])
            return carry

        def stresses(k, carry):
            d = k + 1
            a = A[k, rr]
            b = (0.5 * ELASTIC_STEP) * a
            xx, yy, zz = dx(0, d), dy(1, d), dz(2, d)
            trace = xx + yy + zz
            W[3, d, rr] = a * W[3, d, rr] + b * (trace + 2.0 * xx)
            W[4, d, rr] = a * W[4, d, rr] + b * (trace + 2.0 * yy)
            W[5, d, rr] = a * W[5, d, rr] + b * (trace + 2.0 * zz)
            W[6, d, rr] = a * W[6, d, rr] + b * (dz(1, d) + dy(2, d))
            W[7, d, rr] = a * W[7, d, rr] + b * (dz(0, d) + dx(2, d))
            W[8, d, rr] = a * W[8, d, rr] + b * (dy(0, d) + dx(1, d))
            return carry

        def substep(_, carry):
            lax.fori_loop(0, 2 * depth, velocity, 0)
            lax.fori_loop(0, 2 * depth, stresses, 0)
            return carry

        lax.fori_loop(0, SUBSTEPS, substep, 0)

    spin_step(0, 0, total)

    sent(group_b)
    y_wait(1)
    unpack(late, n_a, halo_lane)
    for d in range(2 * depth):
        B[d, span] = (0.5 * ELASTIC_STEP) * A[d, span] * B[d, span]

    elastic(0, total)
    spin_step(1, 2 * SUBSTEPS, total - 4 * SUBSTEPS)

    far_f = pl.ds(layers * (1 - h), layers)
    far_d = pl.ds(1 + depth * (1 - h), depth)
    film_swap = pltpu.make_async_remote_copy(
        src_ref=F.at[0, :, far_f, pl.ds(own0, rows)], dst_ref=FX, send_sem=os_sem.at[0],
        recv_sem=or_sem.at[0], device_id=partner, device_id_type=MESH)
    film_swap.start()
    elastic(2 * SUBSTEPS, total - 4 * SUBSTEPS)
    wave_swap = pltpu.make_async_remote_copy(
        src_ref=W.at[:, far_d, pl.ds(own0, rows)], dst_ref=WX, send_sem=os_sem.at[1],
        recv_sem=or_sem.at[1], device_id=partner, device_id_type=MESH)
    wave_swap.start()

    mine = lane_own // 64 == h
    film_swap.wait()
    for c in range(3):
        for l in range(layers):
            spin_out[c, l] = jnp.where(mine, F[0, c, f0 + l, own], FX[c, l])
    wave_swap.wait()
    for c in range(9):
        for d in range(depth):
            wave_out[c, d] = jnp.where(mine, W[c, d0 + d, own], WX[c, d])


def body(sizes, wave, buoy, sponge, spin, regions, table):
    depth, rows, lanes = wave.shape[1:]
    layers = spin.shape[1]
    total = rows + 2 * REACH
    tall = total + 2 * PAD
    f32 = lambda *s: pltpu.VMEM(s, jnp.float32)
    dma = lambda *s: pltpu.SemaphoreType.DMA(s)
    n_pk = 3 * 2 * layers // 8 + 2 + (11 * 2 * depth - 8 + 7) // 8
    vmem = pl.BlockSpec(memory_space=pltpu.VMEM)
    return pl.pallas_call(
        functools.partial(kernel, sizes),
        name="film_and_substrate",
        out_shape=(
            jax.ShapeDtypeStruct(wave.shape, jnp.float32),
            jax.ShapeDtypeStruct(spin.shape, jnp.float32),
        ),
        in_specs=[vmem] * 5 + [pl.BlockSpec(memory_space=pltpu.SMEM)],
        out_specs=(vmem, vmem),
        scratch_shapes=[
            f32(9, 2 * depth + 2, tall, lanes),
            f32(2 * depth, tall, lanes),
            pltpu.VMEM((2 * depth, tall, lanes), jnp.int32),
            f32(2 * depth, tall, lanes),
            f32(2, 3, 2 * layers, tall, lanes),
            f32(tall, lanes),
            f32(4, total, lanes),
            f32(6, total, lanes),
            f32(2 * depth, 3, total, lanes),
            f32(n_pk, total, lanes),
            f32(n_pk, total, lanes),
            f32(rows, lanes),
            f32(9, depth, rows, lanes),
            f32(3, layers, rows, lanes),
            dma(7, 2), dma(7, 2), dma(7), dma(7), dma(7, 2), dma(7, 2),
            dma(2), dma(2), dma(2), dma(2), dma(7),
        ],
        compiler_params=pltpu.CompilerParams(
            collective_id=0, has_side_effects=True, vmem_limit_bytes=40 * 2**20),
    )(wave, buoy, sponge, spin, regions, table)


def solution(mesh):
    sizes = (mesh.shape["gx"], mesh.shape["gy"])
    return jax.shard_map(
        functools.partial(body, sizes),
        mesh=mesh,
        in_specs=(
            P("groups", "gz", "gx", "gy"),
            P(("groups", "gz"), "gx", "gy"),
            P(("groups", "gz"), "gx", "gy"),
            P("groups", "gz", "gx", "gy"),
            P(("groups", "gx"), "gy"),
            P(),
        ),
        out_specs=(P("groups", "gz", "gx", "gy"), P("groups", "gz", "gx", "gy")),
        check_vma=False,
    )
```

```python
import functools

import jax
import jax.numpy as jnp
from jax import lax
from jax.experimental import pallas as pl
from jax.experimental.pallas import tpu as pltpu
from jax.sharding import PartitionSpec as P

SUBSTEPS = 4
LLG_STEPS = 2
REACH = 2 * SUBSTEPS * LLG_STEPS
PAD = 8
ELASTIC_STEP = 0.3
SPIN_STEP = 0.04
DAMPING = 0.3
FORCE_SCALE = 0.25
SPONGE_RATE = 0.08
POISSON = 0.2
MESH = pl.DeviceIdType.MESH


def kernel(
    sizes,
    wave, buoy, sponge, spin, regions, table,
    wave_out, spin_out,
    W, B, G, A, F, M, MAT, K, FORCE, PKS, PKR, MOWN, WX, FX,
    xs_sem, xr_sem, ps_sem, pr_sem, fs_sem, fr_sem, ys_sem, yr_sem, os_sem, or_sem, l_sem,
):
    n_x, n_y = sizes
    g = lax.axis_index("groups")
    x = lax.axis_index("gx")
    y = lax.axis_index("gy")
    h = lax.axis_index("gz")
    rows = wave.shape[2]
    halo = REACH
    depth = wave.shape[1]
    layers = spin.shape[1]
    lo0, own0, hi0 = PAD, PAD + halo, PAD + halo + rows
    total = rows + 2 * halo
    span = slice(PAD, PAD + total)
    own = slice(own0, own0 + rows)

    partner = (g, x, y, 1 - h)
    has_lo, has_hi = x > 0, x < n_x - 1
    has_left, has_right = y > 0, y < n_y - 1
    step_y = 1 - 2 * h
    y_to = y + step_y
    y_from = y - step_y
    sends_y = jnp.logical_and(y_to >= 0, y_to < n_y)
    takes_y = jnp.logical_and(y_from >= 0, y_from < n_y)

    barrier = pltpu.get_barrier_semaphore()

    def greet(cond, dev):
        @pl.when(cond)
        def _():
            pl.semaphore_signal(barrier, inc=1, device_id=dev, device_id_type=MESH)

    pl.semaphore_signal(barrier, inc=1, device_id=partner, device_id_type=MESH)
    greet(has_lo, (g, x - 1, y, h))
    greet(has_hi, (g, x + 1, y, h))
    greet(has_left, (g, x, y - 1, h))
    greet(has_right, (g, x, y + 1, h))

    lane_own = lax.broadcasted_iota(jnp.int32, (rows, 128), 1)
    region = jnp.broadcast_to(regions[...], (rows, 128))
    packed = jnp.zeros((rows, 128), jnp.float32)
    for p in range(4):
        value = jnp.zeros((rows, 128), jnp.float32)
        for r in range(table.shape[1]):
            value = jnp.where(region == r, table[p, r], value)
        packed = jnp.where(lane_own // 32 == p, value, packed)
    MOWN[...] = packed

    i32 = lambda c: jnp.where(c, 1, 0).astype(jnp.int32)
    pl.semaphore_wait(barrier, 1 + i32(has_lo) + i32(has_hi) + i32(has_left) + i32(has_right))

    d0 = 1 + depth * h
    b0 = depth * h
    f0 = layers * h

    def piece(i, r):
        rr = pl.ds(r, rows)
        return [
            (spin, F.at[0, :, pl.ds(f0, layers), rr]),
            (MOWN, M.at[rr]),
            (wave.at[3:9, 0:1], W.at[3:9, pl.ds(d0, 1), rr]),
            (wave.at[0:3], W.at[0:3, pl.ds(d0, depth), rr]),
            (wave.at[3:9, 1:depth], W.at[3:9, pl.ds(d0 + 1, depth - 1), rr]),
            (buoy, B.at[pl.ds(b0, depth), rr]),
            (sponge, G.at[pl.ds(b0, depth), rr]),
        ][i]

    count = 7
    with_partner = (0, 2, 3, 4, 5, 6)
    group_a, group_b = (0, 1, 2), (3, 4, 5, 6)

    def x_copy(i, up):
        src, dst = piece(i, lo0 if up else hi0)
        return pltpu.make_async_remote_copy(
            src_ref=src, dst_ref=dst, send_sem=xs_sem.at[i, 0 if up else 1],
            recv_sem=xr_sem.at[i, 0 if up else 1],
            device_id=(g, x + 1 if up else x - 1, y, h), device_id_type=MESH)

    def own_copy(i):
        src, dst = piece(i, own0)
        return pltpu.make_async_remote_copy(
            src_ref=src, dst_ref=dst, send_sem=ps_sem.at[i], recv_sem=pr_sem.at[i],
            device_id=partner, device_id_type=MESH)

    def forward(i, low):
        _, dst = piece(i, lo0 if low else hi0)
        k = 0 if low else 1
        return pltpu.make_async_remote_copy(
            src_ref=dst, dst_ref=dst, send_sem=fs_sem.at[i, k], recv_sem=fr_sem.at[i, k],
            device_id=partner, device_id_type=MESH)

    def local_copy(i):
        src, dst = piece(i, own0)
        return pltpu.make_async_copy(src, dst, l_sem.at[i])

    for i in range(count):
        @pl.when(has_hi)
        def _():
            x_copy(i, True).start()

        @pl.when(has_lo)
        def _():
            x_copy(i, False).start()

    for i in range(count):
        if i in with_partner:
            own_copy(i).start()
        local_copy(i).start()

    zero_row = jnp.zeros((PAD, 128), jnp.float32)

    for c in range(9):
        for d in (0, 1 + 2 * depth):
            W[c, d] = jnp.zeros((total + 2 * PAD, 128), jnp.float32)

    def pad_rows(d, carry):
        for c in range(9):
            W[c, d, 0:PAD] = zero_row
            W[c, d, PAD + total:] = zero_row
        return carry

    lax.fori_loop(1, 1 + 2 * depth, pad_rows, 0)

    def pad_film(l, carry):
        for c in range(3):
            for b in range(2):
                F[b, c, l, 0:PAD] = zero_row
                F[b, c, l, PAD + total:] = zero_row
        return carry

    lax.fori_loop(0, 2 * layers, pad_film, 0)
    @pl.when(jnp.logical_not(takes_y))
    def _():
        PKR[...] = jnp.zeros_like(PKR)

    lane = lax.broadcasted_iota(jnp.int32, (total, 128), 1)
    row = lax.broadcasted_iota(jnp.int32, (total, 128), 0)
    slot = lax.rem(lane // 16 + (1 - h), 8)
    halo_lane = slot == 0
    halo_film = jnp.logical_and(halo_lane, takes_y)

    def arrive(group):
        for i in group:
            @pl.when(has_lo)
            def _():
                x_copy(i, True).wait_recv()
                if i in with_partner:
                    forward(i, True).start()

            @pl.when(has_hi)
            def _():
                x_copy(i, False).wait_recv()
                if i in with_partner:
                    forward(i, False).start()

        for i in group:
            local_copy(i).wait()
            if i in with_partner:
                own_copy(i).wait_recv()

                @pl.when(has_lo)
                def _():
                    forward(i, True).wait_recv()

                @pl.when(has_hi)
                def _():
                    forward(i, False).wait_recv()

    def sent(group):
        for i in group:
            if i in with_partner:
                own_copy(i).wait_send()

            @pl.when(has_hi)
            def _():
                x_copy(i, True).wait_send()
                if i in with_partner:
                    forward(i, False).wait_send()

            @pl.when(has_lo)
            def _():
                x_copy(i, False).wait_send()
                if i in with_partner:
                    forward(i, True).wait_send()

    def fill(refs, cond, r, zero):
        rr = slice(r, r + rows)

        @pl.when(jnp.logical_not(cond))
        def _():
            for ref in refs:
                ref[..., rr, :] = jnp.zeros_like(ref[..., rr, :]) if zero else ref[..., own, :]

    def pack(planes, first):
        for k in range(0, len(planes), 8):
            out = jnp.zeros((total, 128), jnp.float32)
            for j, ref in enumerate(planes[k:k + 8]):
                value = ref[span]
                if j:
                    value = pltpu.roll(value, 16 * j, 1)
                out = jnp.where(slot == j, value, out)
            PKS[first + k // 8] = out

    def unpack(planes, first, mask):
        for k in range(0, len(planes), 8):
            got = PKR[first + k // 8]
            for j, ref in enumerate(planes[k:k + 8]):
                value = pltpu.roll(got, 128 - 16 * j, 1) if j else got
                ref[span] = jnp.where(mask, value, ref[span])

    film_planes = [F.at[0, c, l] for c in range(3) for l in range(2 * layers)]
    stress = range(3, 9)
    first_stress = [W.at[c, 1] for c in stress] + [W.at[c, 1 + depth] for c in stress]
    rest = [W.at[c, 1 + d] for c in range(3) for d in range(2 * depth)]
    rest += [W.at[c, 1 + d] for c in stress for d in range(2 * depth) if d % depth]
    coefs = [B.at[d] for d in range(2 * depth)] + [A.at[d] for d in range(2 * depth)]
    early, late = first_stress[:8], first_stress[8:] + rest + coefs
    n_film = len(film_planes) // 8
    n_a = n_film + 2
    n_b = (len(late) + 7) // 8

    def y_copy(k):
        sl = pl.ds(0, n_a) if k == 0 else pl.ds(n_a, n_b)
        return pltpu.make_async_remote_copy(
            src_ref=PKS.at[sl], dst_ref=PKR.at[sl], send_sem=ys_sem.at[k], recv_sem=yr_sem.at[k],
            device_id=(g, x, y_to, h), device_id_type=MESH)

    def y_start(k):
        @pl.when(sends_y)
        def _():
            y_copy(k).start()

    def y_wait(k):
        @pl.when(sends_y)
        def _():
            y_copy(k).wait_send()

        @pl.when(takes_y)
        def _():
            y_copy(k).wait_recv()

    arrive(group_a)
    for cond, r in ((has_lo, lo0), (has_hi, hi0)):
        fill([F.at[0], M], cond, r, False)
        fill([W.at[3:9, 1:2], W.at[3:9, 1 + depth:2 + depth]], cond, r, True)
    pack(film_planes, 0)
    pack(early, n_film)
    PKS[n_film + 1] = M[span]
    y_start(0)

    arrive(group_b)
    for cond, r in ((has_lo, lo0), (has_hi, hi0)):
        fill([B], cond, r, False)
        fill([W.at[0:3, 1:1 + 2 * depth]], cond, r, True)
        for d in range(2 * depth):
            if d % depth:
                fill([W.at[3:9, 1 + d:2 + d]], cond, r, True)
    inside = jnp.logical_and(
        jnp.logical_or(row >= halo, has_lo), jnp.logical_or(row < halo + rows, has_hi))
    for d in range(2 * depth):
        A[d, span] = jnp.where(inside, 1.0 - SPONGE_RATE * G[d, span].astype(jnp.float32), 0.0)
    pack(late, n_a)
    y_start(1)

    sent(group_a)
    y_wait(0)
    unpack(film_planes, 0, halo_film)
    unpack(early, n_film, halo_lane)
    mine, other = M[span], PKR[n_film + 1]
    for p in range(4):
        at = slice(32 * p, 32 * p + 1)
        MAT[p] = jnp.where(
            halo_film, jnp.broadcast_to(other[:, at], (total, 128)),
            jnp.broadcast_to(mine[:, at], (total, 128)))

    def spin_step(now, r0, n):
        new = 1 - now
        rr, mm = slice(PAD + r0, PAD + r0 + n), slice(r0, r0 + n)
        s = [W[c, 1, rr] for c in stress]
        an, nc, sc = MAT[0, mm], MAT[2, mm], MAT[3, mm]
        part = POISSON * (s[0] + s[1] + s[2])
        K[0, mm] = -6.0 - nc * (s[0] - part)
        K[1, mm] = -6.0 - nc * (s[1] - part)
        K[2, mm] = -6.0 - nc * (s[2] - part) + 2.0 * an
        for q in (3, 4, 5):
            K[q, mm] = -(sc * s[q])
        lanes = lax.broadcasted_iota(jnp.int32, (n, 128), 1)
        at_rows = lax.broadcasted_iota(jnp.int32, (n, 128), 0) + r0
        x_first = jnp.logical_and(at_rows == halo, x == 0)
        x_last = jnp.logical_and(at_rows == halo + rows - 1, x == n_x - 1)
        y_first = jnp.logical_and(lanes == 0, jnp.logical_and(y == 0, h == 0))
        y_last = jnp.logical_and(lanes == 127, jnp.logical_and(y == n_y - 1, h == 1))
        factor = SPIN_STEP / (1.0 + DAMPING * DAMPING)

        def layer(l, sums):
            up, down = min(l + 1, 2 * layers - 1), max(l - 1, 0)
            m, lap, dx, dy = [], [], [], []
            for c in range(3):
                mid = F[now, c, l, rr]
                xp = jnp.where(x_last, mid, F[now, c, l, PAD + r0 + 1:PAD + r0 + 1 + n])
                xm = jnp.where(x_first, mid, F[now, c, l, PAD + r0 - 1:PAD + r0 - 1 + n])
                yp = jnp.where(y_last, mid, pltpu.roll(mid, 127, 1))
                ym = jnp.where(y_first, mid, pltpu.roll(mid, 1, 1))
                m.append(mid)
                lap.append(F[now, c, up, rr] + F[now, c, down, rr] + xp + xm + yp + ym)
                dx.append(xp - xm if c != 1 else None)
                dy.append(yp - ym if c != 0 else None)
            mx, my, mz = m
            half = 0.5 * MAT[1, mm]
            hx = lap[0] + half * dx[2] + K[0, mm] * mx + K[5, mm] * my + K[4, mm] * mz
            hy = lap[1] + half * dy[2] + K[5, mm] * mx + K[1, mm] * my + K[3, mm] * mz
            hz = lap[2] - half * (dx[0] + dy[1]) + K[4, mm] * mx + K[3, mm] * my + K[2, mm] * mz
            tx = my * hz - mz * hy
            ty = mz * hx - mx * hz
            tz = mx * hy - my * hx
            qx = mx - factor * (tx + DAMPING * (my * tz - mz * ty))
            qy = my - factor * (ty + DAMPING * (mz * tx - mx * tz))
            qz = mz - factor * (tz + DAMPING * (mx * ty - my * tx))
            square = qx * qx + qy * qy + qz * qz
            inv = lax.rsqrt(square)
            inv = inv * (1.5 - 0.5 * square * inv * inv)
            qx, qy, qz = qx * inv, qy * inv, qz * inv
            F[new, 0, l, rr] = qx
            F[new, 1, l, rr] = qy
            F[new, 2, l, rr] = qz
            return sums[0] + qx * qz, sums[1] + qy * qz, sums[2] + (qz * qz - 1.0 / 3.0)

        zero = jnp.zeros((n, 128), jnp.float32)
        sums = (zero, zero, zero)
        for l in range(2 * layers):
            sums = layer(l, sums)
        sc, nc = MAT[3, mm], MAT[2, mm]
        FORCE[0, mm] = (2.0 * FORCE_SCALE) * (sc * sums[0])
        FORCE[1, mm] = (2.0 * FORCE_SCALE) * (sc * sums[1])
        FORCE[2, mm] = (2.0 * FORCE_SCALE) * (nc * sums[2])

    def elastic(r0, n):
        lo = PAD + r0
        rr, mm = slice(lo, lo + n), slice(r0, r0 + n)

        def dx(c, d):
            return W[c, d, lo + 1:lo + 1 + n] - W[c, d, lo - 1:lo - 1 + n]

        def dy(c, d):
            value = W[c, d, rr]
            return pltpu.roll(value, 127, 1) - pltpu.roll(value, 1, 1)

        def dz(c, d):
            return W[c, d + 1, rr] - W[c, d - 1, rr]

        def push(k, c):
            return FORCE[c, mm] if k == 0 else 0.0

        def velocity(k, carry):
            d = k + 1
            a, b = A[k, rr], B[k, rr]
            W[0, d, rr] = a * W[0, d, rr] + b * (dx(3, d) + dy(8, d) + dz(7, d) + push(k, 0))
            W[1, d, rr] = a * W[1, d, rr] + b * (dx(8, d) + dy(4, d) + dz(6, d) + push(k, 1))
            W[2, d, rr] = a * W[2, d, rr] + b * (dx(7, d) + dy(6, d) + dz(5, d) + push(k, 2))
            return carry

        def stresses(k, carry):
            d = k + 1
            a = A[k, rr]
            b = (0.5 * ELASTIC_STEP) * a
            xx, yy, zz = dx(0, d), dy(1, d), dz(2, d)
            trace = xx + yy + zz
            W[3, d, rr] = a * W[3, d, rr] + b * (trace + 2.0 * xx)
            W[4, d, rr] = a * W[4, d, rr] + b * (trace + 2.0 * yy)
            W[5, d, rr] = a * W[5, d, rr] + b * (trace + 2.0 * zz)
            W[6, d, rr] = a * W[6, d, rr] + b * (dz(1, d) + dy(2, d))
            W[7, d, rr] = a * W[7, d, rr] + b * (dz(0, d) + dx(2, d))
            W[8, d, rr] = a * W[8, d, rr] + b * (dy(0, d) + dx(1, d))
            return carry

        def substep(_, carry):
            for k in range(2 * depth):
                velocity(k, 0)
            for k in range(2 * depth):
                stresses(k, 0)
            return carry

        lax.fori_loop(0, SUBSTEPS, substep, 0)

    spin_step(0, 0, total)

    sent(group_b)
    y_wait(1)
    unpack(late, n_a, halo_lane)
    for d in range(2 * depth):
        B[d, span] = (0.5 * ELASTIC_STEP) * A[d, span] * B[d, span]

    elastic(0, total)
    spin_step(1, 2 * SUBSTEPS, total - 4 * SUBSTEPS)

    far_f = pl.ds(layers * (1 - h), layers)
    far_d = pl.ds(1 + depth * (1 - h), depth)
    film_swap = pltpu.make_async_remote_copy(
        src_ref=F.at[0, :, far_f, pl.ds(own0, rows)], dst_ref=FX, send_sem=os_sem.at[0],
        recv_sem=or_sem.at[0], device_id=partner, device_id_type=MESH)
    film_swap.start()
    elastic(2 * SUBSTEPS, total - 4 * SUBSTEPS)
    wave_swap = pltpu.make_async_remote_copy(
        src_ref=W.at[:, far_d, pl.ds(own0, rows)], dst_ref=WX, send_sem=os_sem.at[1],
        recv_sem=or_sem.at[1], device_id=partner, device_id_type=MESH)
    wave_swap.start()

    mine = lane_own // 64 == h
    film_swap.wait()
    for c in range(3):
        for l in range(layers):
            spin_out[c, l] = jnp.where(mine, F[0, c, f0 + l, own], FX[c, l])
    wave_swap.wait()
    for c in range(9):
        for d in range(depth):
            wave_out[c, d] = jnp.where(mine, W[c, d0 + d, own], WX[c, d])


def body(sizes, wave, buoy, sponge, spin, regions, table):
    depth, rows, lanes = wave.shape[1:]
    layers = spin.shape[1]
    total = rows + 2 * REACH
    tall = total + 2 * PAD
    f32 = lambda *s: pltpu.VMEM(s, jnp.float32)
    dma = lambda *s: pltpu.SemaphoreType.DMA(s)
    n_pk = 3 * 2 * layers // 8 + 2 + (11 * 2 * depth - 8 + 7) // 8
    vmem = pl.BlockSpec(memory_space=pltpu.VMEM)
    return pl.pallas_call(
        functools.partial(kernel, sizes),
        name="film_and_substrate",
        out_shape=(
            jax.ShapeDtypeStruct(wave.shape, jnp.float32),
            jax.ShapeDtypeStruct(spin.shape, jnp.float32),
        ),
        in_specs=[vmem] * 5 + [pl.BlockSpec(memory_space=pltpu.SMEM)],
        out_specs=(vmem, vmem),
        scratch_shapes=[
            f32(9, 2 * depth + 2, tall, lanes),
            f32(2 * depth, tall, lanes),
            pltpu.VMEM((2 * depth, tall, lanes), jnp.int32),
            f32(2 * depth, tall, lanes),
            f32(2, 3, 2 * layers, tall, lanes),
            f32(tall, lanes),
            f32(4, total, lanes),
            f32(6, total, lanes),
            f32(3, total, lanes),
            f32(n_pk, total, lanes),
            f32(n_pk, total, lanes),
            f32(rows, lanes),
            f32(9, depth, rows, lanes),
            f32(3, layers, rows, lanes),
            dma(7, 2), dma(7, 2), dma(7), dma(7), dma(7, 2), dma(7, 2),
            dma(2), dma(2), dma(2), dma(2), dma(7),
        ],
        compiler_params=pltpu.CompilerParams(
            collective_id=0, has_side_effects=True, vmem_limit_bytes=40 * 2**20),
    )(wave, buoy, sponge, spin, regions, table)


def solution(mesh):
    sizes = (mesh.shape["gx"], mesh.shape["gy"])
    return jax.shard_map(
        functools.partial(body, sizes),
        mesh=mesh,
        in_specs=(
            P("groups", "gz", "gx", "gy"),
            P(("groups", "gz"), "gx", "gy"),
            P(("groups", "gz"), "gx", "gy"),
            P("groups", "gz", "gx", "gy"),
            P(("groups", "gx"), "gy"),
            P(),
        ),
        out_specs=(P("groups", "gz", "gx", "gy"), P("groups", "gz", "gx", "gy")),
        check_vma=False,
    )
```
